256 devices in a mesh: mz: 32 (over z, y), rt: 4 (over x), samp: 2 (over core).
Axes of the slice: x: 4, y: 4, z: 8, core: 2. Of those that a mesh axis runs over, the one named last changes fastest.
Arguments:
- spectra: float32 [8, 2048, 16384], P('samp', 'rt', 'mz'), may hold values from -120 to 120
- sample_factor: float32 [32, 8], P(None, 'samp'), may hold values from 0.2 to 1
- scan_factor: float32 [32, 2048], P('mz', 'rt'), may hold values from -0.125 to 0.125
Outputs:
- mz_factor: float32 [32, 16384], P(None, ('mz', 'rt', 'samp'))
- peak_scales: float32 [32], replicated
- factor_gram: float32 [32, 32], replicated
The draws below stay inside these ranges and needn't reach their ends.
All inputs are finite; a program needn't handle non-finite values. Where the reference program divides by a largest or mean magnitude, that divisor is 1e-20 or more.
Results may differ from the reference program's by a relative error of at most 0.00014.
Values sent between devices are 32-bit elements; how exact they have to be, the bound alone decides.
No kernel may reach another device: no remote copies, remote signals or barrier semaphores. Data moves between devices by JAX's collectives and lax.ppermute only.
A program may use at most 64 MiB of HBM per device.

```python
import math
import jax
import jax.numpy as jnp
from jax import lax

RANK = 32
MZ = 16384
SAMPLES = 8
SCANS = 2048


def draw_spectra(key, part):
    key = jax.random.fold_in(key, 11)
    sample_key = jax.random.fold_in(key, 1)
    scan_key = jax.random.fold_in(key, 2)
    bin_key = jax.random.fold_in(key, 3)
    base_key = jax.random.fold_in(key, 4)
    top = math.log(10.0)
    sample_scale = jnp.exp(jax.random.uniform(sample_key, (SAMPLES, 1, 1), jnp.float32, 0.0, top))
    scan_scale = jnp.exp(jax.random.uniform(scan_key, (1, SCANS, 1), jnp.float32, 0.0, top))
    trend = jnp.exp(math.log(3.0) * jnp.arange(MZ, dtype=jnp.float32) / MZ)
    bin_scale = jnp.exp(jax.random.uniform(bin_key, (1, 1, MZ), jnp.float32, 0.0, top)) * trend[None, None, :]
    base = jax.random.truncated_normal(base_key, -4.0, 4.0, (SAMPLES, SCANS, MZ), jnp.float32)
    return (0.01 * base * sample_scale * scan_scale * bin_scale).astype(jnp.float32)


def level_of(stream_key, shape, pieces, smallest, top_value):
    def one(dim, shards_of):
        draws = jax.random.uniform(jax.random.fold_in(jax.random.fold_in(stream_key, 6), dim), (shards_of,), jnp.float32, smallest / len(pieces), top_value / len(pieces))
        return jnp.repeat(jnp.exp(draws), shape[dim] // shards_of).reshape((-1,) + (1,) * (len(shape) - dim - 1))

    gain = one(*pieces[0])
    for cut in pieces[1:]:
        gain = gain * one(*cut)
    return gain


def centred(rng, extent, scale, reach, cuts=(), kind=jnp.bfloat16):
    level = level_of(rng, extent, cuts, -0.22, 0.18) if cuts else 1.0
    drawn = jax.random.normal(rng, extent, jnp.float32) * scale * level
    return jnp.minimum(jnp.maximum(drawn, -reach), reach).astype(kind)


def setup_inputs(seed: int = 0) -> dict:
    streams_of = jax.random.split(jax.random.key(seed), 4)
    return {
        "spectra": draw_spectra(jax.random.fold_in(streams_of[3], 71), 0),
        "sample_factor": jnp.clip(0.2 + 0.8 * jax.random.uniform(streams_of[1], (RANK, SAMPLES), jnp.float32) ** level_of(streams_of[1], (RANK, SAMPLES), ((1, 2),), -0.2, 0.2), 0.2, 1.0),
        "scan_factor": centred(streams_of[2], (RANK, SCANS), SCANS ** -0.5, 0.125, ((0, 32), (1, 4)), jnp.float32),
    }


def reference(spectra, sample_factor, scan_factor):
    highest = lax.Precision.HIGHEST
    gram_sample = jnp.dot(sample_factor, sample_factor.T, precision=highest)
    gram_scan = jnp.dot(scan_factor, scan_factor.T, precision=highest)
    system = gram_sample * gram_scan
    khatri = (sample_factor[:, :, None] * scan_factor[:, None, :]).reshape(RANK, SAMPLES * SCANS)
    product = jnp.dot(khatri, spectra.reshape(SAMPLES * SCANS, MZ), precision=highest)
    chol_lower = jnp.linalg.cholesky(system)
    raw_factor = jax.scipy.linalg.cho_solve((chol_lower, True), product)
    peak_scales = jnp.max(jnp.abs(raw_factor), axis=1) + 1e-06
    mz_factor = raw_factor / peak_scales[:, None]
    factor_gram = jnp.dot(mz_factor, mz_factor.T, precision=highest) / MZ
    return (mz_factor, peak_scales, factor_gram)
```

```python
import jax
import jax.numpy as jnp
from jax import lax
from jax.experimental import pallas as pl
from jax.experimental.pallas import tpu as pltpu
from jax.sharding import PartitionSpec as P

MZ = 16384
RANK = 32
HIGHEST = lax.Precision.HIGHEST
F32 = jnp.float32
VMEM = pl.BlockSpec(memory_space=pltpu.VMEM)


def iota(shape, dim):
    return lax.broadcasted_iota(jnp.int32, shape, dim)


def split(x):
    high = x.astype(jnp.bfloat16)
    return high, (x - high.astype(F32)).astype(jnp.bfloat16)


def nt_dot(a, b):
    return lax.dot_general(
        a, b, (((1,), (1,)), ((), ())), precision=HIGHEST, preferred_element_type=F32
    )


def contract_kernel(spectra_ref, sample_ref, scan_ref, keep_ref, send_ref, buffer, sems):
    count = spectra_ref.shape[0]
    copies = [
        pltpu.make_async_copy(spectra_ref.at[s], buffer.at[s], sems.at[s]) for s in range(count)
    ]
    for copy in copies:
        copy.start()
    scan = scan_ref[...]
    sample = sample_ref[...]
    gram = nt_dot(scan, scan)
    scan_high, scan_low = split(scan)
    stacked = jnp.concatenate([scan_high, scan_low], axis=0)
    total = jnp.zeros((RANK, spectra_ref.shape[2]), F32)
    for s in range(count):
        copies[s].wait()
        high, low = split(buffer[s])
        both = jnp.dot(stacked, high, preferred_element_type=F32)
        part = both[:RANK] + both[RANK:] + jnp.dot(scan_high, low, preferred_element_type=F32)
        total = total + sample[:, s : s + 1] * part
    core = lax.axis_index("samp")
    first = iota((RANK, 128), 1) < 64
    halves = ([], [])
    for t in range(0, 4, 2):
        a, b = total[:, t * 128 : (t + 1) * 128], total[:, (t + 1) * 128 : (t + 2) * 128]
        halves[0].append(jnp.where(first, a, pltpu.roll(b, 64, 1)))
        halves[1].append(jnp.where(first, pltpu.roll(a, 64, 1), b))
    for t in range(2):
        cut = slice(t * 128, (t + 1) * 128)
        keep_ref[:, cut] = jnp.where(core == 0, halves[0][t], halves[1][t])
        send_ref[:, cut] = jnp.where(core == 0, halves[1][t], halves[0][t])
    keep_ref[:, 256:] = jnp.zeros((RANK, 128), F32)
    send_ref[:, 256:] = jnp.zeros((RANK, 128), F32)
    keep_ref[:, 256 : 256 + RANK] = gram
    send_ref[:, 256 : 256 + count] = sample


def packed_index(count):
    place = iota((RANK, count), 1)
    whole = place < 512
    row = jnp.where(whole, place >> 5, 16 + ((place - 512) >> 4))
    column = jnp.where(whole, place & 31, 16 + (place & 15))
    return row, column


def solve_kernel(mine_ref, other_ref, sample_ref, sample_other_ref, raw_ref, packet_ref):
    own, away = sample_ref[...], sample_other_ref[:, 256 : 256 + sample_ref.shape[1]]
    system = (nt_dot(own, own) + nt_dot(away, away)) * mine_ref[:, 256 : 256 + RANK]
    parts = [mine_ref[:, :256], other_ref[...]]
    row_of = iota((RANK, 1), 0)
    for k in range(RANK):
        here = row_of == k
        scale = 1.0 / system[k : k + 1, k : k + 1]
        column = jnp.where(here, -1.0, system[:, k : k + 1])
        parts = [
            jnp.where(here, 0.0, part) - column * (part[k : k + 1] * scale) for part in parts
        ]
        system = jnp.where(here, 0.0, system) - column * (system[k : k + 1] * scale)
    slot = lax.axis_index("rt")
    pair = jnp.where(slot < 2, parts[0][:, :128], parts[0][:, 128:])
    raw_ref[...] = jnp.where(slot % 2 == 0, pair, pltpu.roll(pair, 64, 1))[:, :64]
    peak = jnp.maximum(*(jnp.max(jnp.abs(part), axis=1, keepdims=True) for part in parts)) + 1e-06
    scaled = [part / peak for part in parts]
    gram = nt_dot(scaled[0], scaled[0]) + nt_dot(scaled[1], scaled[1])
    row, column = packed_index(768)
    spread = jnp.where(iota((RANK, 768), 0) == column, 1.0, 0.0)
    flat = jnp.dot(gram, spread, precision=HIGHEST, preferred_element_type=F32)
    flat = jnp.sum(jnp.where(iota((RANK, 768), 0) == row, flat, 0.0), axis=0, keepdims=True)
    lane = iota((RANK, 128), 1)
    peak_row = jnp.sum(jnp.where(lane == row_of, peak, 0.0), axis=0, keepdims=True)
    packet = jnp.concatenate(
        [flat[:, u * 128 : (u + 1) * 128] for u in range(6)] + [peak_row, jnp.zeros((1, 128), F32)],
        axis=0,
    )
    for d in range(packet_ref.shape[0]):
        packet_ref[d] = packet


def finish_kernel(packets_ref, raw_ref, factor_ref, peak_ref, gram_ref):
    peaks = packets_ref[:, 6, :RANK]
    peak_row = jnp.max(peaks, axis=0, keepdims=True)
    ratio = peaks / peak_row
    row, column = packed_index(768)
    component = iota((RANK, 768), 0)
    of_row, of_column = component == row, component == column
    row_scale = jnp.dot(
        ratio, jnp.where(of_row, 1.0, 0.0), precision=HIGHEST, preferred_element_type=F32
    )
    column_scale = jnp.dot(
        ratio, jnp.where(of_column, 1.0, 0.0), precision=HIGHEST, preferred_element_type=F32
    )
    packed = jnp.concatenate([packets_ref[:, u, :] for u in range(6)], axis=1)
    flat = jnp.sum(packed * row_scale * column_scale, axis=0, keepdims=True) * (1.0 / MZ)
    gram = nt_dot(jnp.where(of_row, flat, 0.0), jnp.where(of_column, 1.0, 0.0))
    place = iota((RANK, 768), 1)
    corner = (place < 512) & (column >= 16)
    gram = gram + nt_dot(
        jnp.where(of_column & corner, flat, 0.0), jnp.where(of_row & corner, 1.0, 0.0)
    )
    peak_ref[...] = peak_row
    diagonal = iota((RANK, RANK), 0) == iota((RANK, RANK), 1)
    peak = jnp.sum(jnp.where(diagonal, peak_row, 0.0), axis=1, keepdims=True)
    factor_ref[...] = raw_ref[...] / peak
    gram_ref[...] = gram


def call(kernel, shapes, ins, scratch=(), name=None):
    return pl.pallas_call(
        kernel,
        out_shape=[jax.ShapeDtypeStruct(s, F32) for s in shapes],
        in_specs=ins,
        out_specs=[VMEM] * len(shapes),
        scratch_shapes=list(scratch),
        compiler_params=pltpu.CompilerParams(vmem_limit_bytes=32 * 1024 * 1024),
        name=name,
    )


def shift(x, axis, size, by):
    return lax.ppermute(x, axis, [(i, (i + by) % size) for i in range(size)])


def local(spectra, sample_factor, scan_factor):
    bins = spectra.shape[2]
    rows = jnp.broadcast_to(scan_factor[None], (RANK, 1, scan_factor.shape[1]))
    scan_block = lax.all_to_all(rows, "mz", 0, 0).reshape(RANK, scan_factor.shape[1])
    half = bins // 2
    keep, send = call(
        contract_kernel,
        [(RANK, half + 128)] * 2,
        [pl.BlockSpec(memory_space=pl.ANY), VMEM, VMEM],
        [pltpu.VMEM(spectra.shape, F32), pltpu.SemaphoreType.DMA((spectra.shape[0],))],
        "contract",
    )(spectra, sample_factor, scan_block)
    taken = shift(send, "samp", 2, 1)
    lane = iota(keep.shape, 1)
    partial = keep + jnp.where(lane < half, taken, 0.0)
    far = [shift(partial, "rt", 4, by) for by in (1, 2, 3)]
    mine = (partial + far[1]) + (far[0] + far[2])
    other = shift(mine[:, :half], "samp", 2, 1)
    raw, packets = call(
        solve_kernel, [(RANK, 64), (RANK, 8, 128)], [VMEM] * 4, name="solve"
    )(mine, other, sample_factor, taken)
    packets = lax.all_to_all(packets, "mz", 0, 0)
    factor, peak, gram = call(
        finish_kernel, [(RANK, 64), (1, RANK), (RANK, RANK)], [VMEM] * 2, name="finish"
    )(packets, raw)
    return (factor, peak.reshape(RANK), gram)


def solution(mesh):
    return jax.shard_map(
        local,
        mesh=mesh,
        in_specs=(P("samp", "rt", "mz"), P(None, "samp"), P("mz", "rt")),
        out_specs=(P(None, ("mz", "rt", "samp")), P(), P()),
        check_vma=False,
    )
```

```python
import jax
import jax.numpy as jnp
from jax import lax
from jax.experimental import pallas as pl
from jax.experimental.pallas import tpu as pltpu
from jax.sharding import PartitionSpec as P

MZ = 16384
RANK = 32
BINS = 512
HIGHEST = lax.Precision.HIGHEST
F32 = jnp.float32
BF16 = jnp.bfloat16
VMEM = pl.BlockSpec(memory_space=pltpu.VMEM)


def iota(shape, dim):
    return lax.broadcasted_iota(jnp.int32, shape, dim)


def split(x):
    high = x.astype(BF16)
    return high, (x - high.astype(F32)).astype(BF16)


def dot(a, b):
    return jnp.dot(a, b, precision=HIGHEST, preferred_element_type=F32)


def nt_dot(a, b):
    return lax.dot_general(
        a, b, (((1,), (1,)), ((), ())), precision=HIGHEST, preferred_element_type=F32
    )


def as_column(row):
    n = row.shape[1]
    return jnp.sum(jnp.where(iota((n, n), 0) == iota((n, n), 1), row, 0.0), axis=1, keepdims=True)


def contract_kernel(spectra_ref, gathered_ref, out_ref):
    scan = jnp.concatenate([gathered_ref[:, u, :] for u in range(4)], axis=1)
    scan_high, scan_low = split(scan)
    stacked = jnp.concatenate([scan_high, scan_low], axis=0)
    last = gathered_ref.shape[0] - 1
    swapped = lax.axis_index("mz") == last
    total = jnp.zeros((RANK, BINS), F32)
    gram = jnp.zeros((RANK, RANK), F32)
    for s in range(spectra_ref.shape[0]):
        one, two = (gathered_ref[d, 4 + s : 5 + s, :RANK] for d in (0, last))
        one_column, two_column = as_column(one), as_column(two)
        gram = gram + (one_column * one + two_column * two)
        high, low = split(spectra_ref[s])
        both = jnp.dot(stacked, high, preferred_element_type=F32)
        part = both[:RANK] + both[RANK:] + jnp.dot(scan_high, low, preferred_element_type=F32)
        total = total + jnp.where(swapped, one_column, two_column) * part
    out_ref[:, :BINS] = total
    out_ref[:, BINS:] = jnp.zeros((RANK, 128), F32)
    out_ref[:, BINS : BINS + RANK] = gram * nt_dot(scan, scan)


def invert_kernel(total_ref, out_ref):
    system = total_ref[:, BINS : BINS + RANK]
    tiles = RANK // 8
    columns = [
        [jnp.broadcast_to(system[8 * t : 8 * t + 8, j : j + 1], (8, 128)) for t in range(tiles)]
        for j in range(RANK)
    ]
    row, lane = iota((8, 128), 0), iota((8, 128), 1)
    work = [jnp.where(row + 8 * t == lane, 1.0, 0.0) for t in range(tiles)]
    pivots = [jnp.ones((8, 128), F32)] * tiles
    for k in range(RANK):
        top, r = divmod(k, 8)
        pivot = columns[k][top][r : r + 1]
        pivots[top] = jnp.where(row == r, pivot, pivots[top])
        scale = 1.0 / pivot
        factor = [columns[k][t] * scale if t >= top else None for t in range(tiles)]
        factor[top] = jnp.where(row > r, factor[top], 0.0)
        pivot_row = work[top][r : r + 1]
        for t in range(top, tiles):
            work[t] = work[t] - factor[t] * pivot_row
            for j in range(k + 1, min(8 * t + 8, RANK)):
                other = columns[k][j // 8][j % 8 : j % 8 + 1]
                columns[j][t] = columns[j][t] - factor[t] * other
    for t in range(tiles):
        out_ref[8 * t : 8 * t + 8] = (work[t] * lax.rsqrt(pivots[t]))[:, :RANK]


def packed_index(count):
    place = iota((RANK, count), 1)
    whole = place < 512
    row = jnp.where(whole, place >> 5, 16 + ((place - 512) >> 4))
    column = jnp.where(whole, place & 31, 16 + (place & 15))
    return row, column


def solve_kernel(mine_ref, other_ref, factor_ref, raw_ref, packet_ref):
    product = mine_ref[:, :BINS] + other_ref[:, :BINS]
    factor = factor_ref[...]
    raw = dot(factor.T, dot(factor, product))
    slot, core = lax.axis_index("rt"), lax.axis_index("samp")
    tiles = [raw[:, t * 128 : (t + 1) * 128] for t in range(4)]
    own = jnp.where(
        slot < 2,
        jnp.where(slot == 0, tiles[0], tiles[1]),
        jnp.where(slot == 2, tiles[2], tiles[3]),
    )
    raw_ref[...] = jnp.where(core == 0, own, pltpu.roll(own, 64, 1))[:, :64]
    peak = jnp.max(jnp.abs(raw), axis=1, keepdims=True) + 1e-06
    scaled = raw * (1.0 / peak)
    gram = nt_dot(scaled, scaled)
    row, column = packed_index(768)
    spread = jnp.where(iota((RANK, 768), 0) == column, 1.0, 0.0)
    flat = dot(gram, spread)
    flat = jnp.sum(jnp.where(iota((RANK, 768), 0) == row, flat, 0.0), axis=0, keepdims=True)
    lane = iota((RANK, 128), 1)
    peak_row = jnp.sum(
        jnp.where(lane == iota((RANK, 128), 0), peak, 0.0), axis=0, keepdims=True
    )
    packet = jnp.concatenate(
        [flat[:, u * 128 : (u + 1) * 128] for u in range(6)] + [peak_row, jnp.zeros((1, 128), F32)],
        axis=0,
    )
    for d in range(packet_ref.shape[0]):
        packet_ref[d] = packet


def finish_kernel(packets_ref, raw_ref, factor_ref, peak_ref, gram_ref):
    peaks = packets_ref[:, 6, :RANK]
    peak_row = jnp.max(peaks, axis=0, keepdims=True)
    ratio = peaks / peak_row
    row, column = packed_index(768)
    component = iota((RANK, 768), 0)
    of_row, of_column = component == row, component == column
    row_scale = dot(ratio, jnp.where(of_row, 1.0, 0.0))
    column_scale = dot(ratio, jnp.where(of_column, 1.0, 0.0))
    packed = jnp.concatenate([packets_ref[:, u, :] for u in range(6)], axis=1)
    flat = jnp.sum(packed * row_scale * column_scale, axis=0, keepdims=True) * (1.0 / MZ)
    gram = nt_dot(jnp.where(of_row, flat, 0.0), jnp.where(of_column, 1.0, 0.0))
    place = iota((RANK, 768), 1)
    corner = (place < 512) & (column >= 16)
    gram = gram + nt_dot(
        jnp.where(of_column & corner, flat, 0.0), jnp.where(of_row & corner, 1.0, 0.0)
    )
    peak_ref[...] = peak_row
    factor_ref[...] = raw_ref[...] / as_column(peak_row)
    gram_ref[...] = gram


def call(kernel, shapes, ins, name=None):
    return pl.pallas_call(
        kernel,
        out_shape=[jax.ShapeDtypeStruct(s, F32) for s in shapes],
        in_specs=ins,
        out_specs=[VMEM] * len(shapes),
        compiler_params=pltpu.CompilerParams(vmem_limit_bytes=24 * 1024 * 1024),
        name=name,
    )


def shift(x, axis, size, by):
    return lax.ppermute(x, axis, [(i, (i + by) % size) for i in range(size)])


def mixed_groups(chips, slots):
    return [
        [
            (chip * slots + slot) * 2 + (core if chip < chips - 1 else 1 - core)
            for chip in range(chips)
        ]
        for slot in range(slots)
        for core in range(2)
    ]


def local(spectra, sample_factor, scan_factor):
    spectra_other = shift(spectra, "samp", 2, 1)
    sample = jnp.pad(sample_factor.T, ((0, 0), (0, 128 - RANK)))
    packet = jnp.concatenate([scan_factor.reshape(4, 128), sample], axis=0)
    gathered = lax.all_to_all(
        jnp.broadcast_to(packet[None], (RANK,) + packet.shape),
        ("mz", "rt", "samp"),
        0,
        0,
        axis_index_groups=mixed_groups(RANK, 4),
    )
    (partial,) = call(contract_kernel, [(RANK, BINS + 128)], [VMEM] * 2, name="contract")(
        spectra_other, gathered
    )
    far = [shift(partial, "rt", 4, by) for by in (1, 3, 2)]
    mine = (partial + far[2]) + (far[0] + far[1])
    other = shift(mine, "samp", 2, 1)
    (factor,) = call(invert_kernel, [(RANK, RANK)], [VMEM], name="invert")(mine)
    raw, packets = call(solve_kernel, [(RANK, 64), (RANK, 8, 128)], [VMEM] * 3, name="solve")(
        mine, other, factor
    )
    packets = lax.all_to_all(packets, "mz", 0, 0)
    factor, peak, gram = call(
        finish_kernel, [(RANK, 64), (1, RANK), (RANK, RANK)], [VMEM] * 2, name="finish"
    )(packets, raw)
    return (factor, peak.reshape(RANK), gram)


def solution(mesh):
    return jax.shard_map(
        local,
        mesh=mesh,
        in_specs=(P("samp", "rt", "mz"), P(None, "samp"), P("mz", "rt")),
        out_specs=(P(None, ("mz", "rt", "samp")), P(), P()),
        check_vma=False,
    )
```

```python
import jax
import jax.numpy as jnp
from jax import lax
from jax.experimental import pallas as pl
from jax.experimental.pallas import tpu as pltpu
from jax.sharding import PartitionSpec as P

MZ = 16384
RANK = 32
BINS = 512
FIRST = 18
HIGHEST = lax.Precision.HIGHEST
F32 = jnp.float32
BF16 = jnp.bfloat16
VMEM = pl.BlockSpec(memory_space=pltpu.VMEM)


def iota(shape, dim):
    return lax.broadcasted_iota(jnp.int32, shape, dim)


def split(x):
    high = x.astype(BF16)
    return high, (x - high.astype(F32)).astype(BF16)


def dot(a, b):
    return jnp.dot(a, b, precision=HIGHEST, preferred_element_type=F32)


def nt_dot(a, b, precision=HIGHEST):
    return lax.dot_general(
        a, b, (((1,), (1,)), ((), ())), precision=precision, preferred_element_type=F32
    )


def as_column(row):
    n = row.shape[1]
    return jnp.sum(jnp.where(iota((n, n), 0) == iota((n, n), 1), row, 0.0), axis=1, keepdims=True)


def dist(a, b):
    z, y = abs(a // 4 - b // 4), abs(a % 4 - b % 4)
    return min(z, 8 - z) + min(y, 4 - y)


def ordered(key):
    return [FIRST] + sorted([c for c in range(RANK) if c != FIRST], key=key)


ORDER_A = [(FIRST + i) % RANK for i in range(RANK)]
ORDER_C = ordered(lambda chip: dist(chip, 0))


def in_order(x):
    place = [ORDER_A.index(chip) for chip in range(RANK)]
    pieces, start = [], 0
    for i in range(1, RANK + 1):
        if i == RANK or place[i] != place[i - 1] + 1:
            pieces.append(x[place[start] : place[start] + i - start])
            start = i
    return jnp.concatenate(pieces, axis=0) if len(pieces) > 1 else x


def contract_kernel(spectra_ref, gathered_ref, out_ref):
    scan = jnp.concatenate([gathered_ref[:, u, :] for u in range(4)], axis=1)
    scan = in_order(scan)
    scan_high, scan_low = split(scan)
    stacked = jnp.concatenate([scan_high, scan_low], axis=0)
    last = gathered_ref.shape[0] - 1
    swapped = lax.axis_index("mz") == ORDER_A[-1]
    total = jnp.zeros((RANK, BINS), F32)
    gram = jnp.zeros((RANK, RANK), F32)
    for s in range(spectra_ref.shape[0]):
        one, two = (gathered_ref[d, 4 + s : 5 + s, :RANK] for d in (0, last))
        one_column, two_column = as_column(one), as_column(two)
        gram = gram + (one_column * one + two_column * two)
        high, low = split(spectra_ref[s])
        both = jnp.dot(stacked, high, preferred_element_type=F32)
        part = both[:RANK] + both[RANK:] + jnp.dot(scan_high, low, preferred_element_type=F32)
        total = total + jnp.where(swapped, one_column, two_column) * part
    out_ref[:, :BINS] = total
    out_ref[:, BINS:] = jnp.zeros((RANK, 128), F32)
    out_ref[:, BINS : BINS + RANK] = gram * nt_dot(scan, scan)


def invert_kernel(total_ref, out_ref):
    system = total_ref[:, BINS : BINS + RANK]
    tiles = RANK // 8
    columns = [
        [jnp.broadcast_to(system[8 * t : 8 * t + 8, j : j + 1], (8, 128)) for t in range(tiles)]
        for j in range(RANK)
    ]
    row, lane = iota((8, 128), 0), iota((8, 128), 1)
    work = [jnp.where(row + 8 * t == lane, 1.0, 0.0) for t in range(tiles)]
    pivots = [jnp.ones((8, 128), F32)] * tiles
    for k in range(RANK):
        top, r = divmod(k, 8)
        pivot = columns[k][top][r : r + 1]
        pivots[top] = jnp.where(row == r, pivot, pivots[top])
        scale = 1.0 / pivot
        factor = [columns[k][t] * scale if t >= top else None for t in range(tiles)]
        factor[top] = jnp.where(row > r, factor[top], 0.0)
        pivot_row = work[top][r : r + 1]
        for t in range(top, tiles):
            work[t] = work[t] - factor[t] * pivot_row
            for j in range(k + 1, min(8 * t + 8, RANK)):
                other = columns[k][j // 8][j % 8 : j % 8 + 1]
                columns[j][t] = columns[j][t] - factor[t] * other
    factor = jnp.concatenate(
        [(work[t] * lax.rsqrt(pivots[t]))[:, :RANK] for t in range(tiles)], axis=0
    )
    out_ref[...] = dot(factor.T, factor)


def solve_kernel(mine_ref, other_ref, inverse_ref, raw_ref, packet_ref):
    raw = dot(inverse_ref[...], mine_ref[:, :BINS] + other_ref[:, :BINS])
    slot, core = lax.axis_index("rt"), lax.axis_index("samp")
    tiles = [raw[:, t * 128 : (t + 1) * 128] for t in range(4)]
    own = jnp.where(
        slot < 2,
        jnp.where(slot == 0, tiles[0], tiles[1]),
        jnp.where(slot == 2, tiles[2], tiles[3]),
    )
    raw_ref[...] = jnp.where(core == 0, own, pltpu.roll(own, 64, 1))[:, :64]
    peak = jnp.max(jnp.abs(raw), axis=1, keepdims=True) + 1e-06
    high, low = split(raw * (1.0 / peak))
    both = nt_dot(jnp.concatenate([high, low], axis=0), high, None)
    gram = both[:RANK] + both[RANK:] + nt_dot(high, low, None)
    diagonal = iota((RANK, RANK), 0) == iota((RANK, RANK), 1)
    peak_row = jnp.sum(jnp.where(diagonal, peak, 0.0), axis=0, keepdims=True)
    packet = jnp.concatenate(
        [gram[:8], gram[8:16], gram[16:24, 16:], gram[24:, 16:], jnp.broadcast_to(peak_row, (8, RANK))],
        axis=1,
    )
    for d in range(packet_ref.shape[0]):
        packet_ref[d] = packet


def take_lanes(x, lanes):
    return jnp.take_along_axis(x, lanes, axis=1, mode="promise_in_bounds")


def finish_kernel(packets_ref, raw_ref, factor_ref, peak_ref, gram_ref):
    count = packets_ref.shape[0]
    peaks = packets_ref[0]
    for d in range(1, count):
        peaks = jnp.maximum(peaks, packets_ref[d])
    scale = 1.0 / peaks
    row, lane = iota((8, 128), 0), iota((8, 128), 1)
    block = jnp.where(lane < 64, lane >> 5, jnp.where(lane < 80, 2, 3))
    of_row = 96 + 8 * block + row
    of_column = 96 + jnp.where(lane < 64, lane & 31, 16 + (lane & 15))
    total = jnp.zeros((8, 128), F32)
    for d in range(count):
        packet = packets_ref[d]
        ratio = packet * scale
        total = total + packet * take_lanes(ratio, of_row) * take_lanes(ratio, of_column)
    total = total * (1.0 / MZ)
    peak_ref[...] = peaks[:1, 96:]
    for t in range(RANK // 8):
        rows = slice(8 * t, 8 * t + 8)
        factor_ref[rows] = raw_ref[rows] / take_lanes(peaks, 96 + 8 * t + row)[:, :64]
    upper = jnp.concatenate([total[:, :32], total[:, 32:64]], axis=0)
    corner = jnp.concatenate([total[:, 64:80], total[:, 80:96]], axis=0)
    gram_ref[:16] = upper
    gram_ref[16:] = jnp.concatenate([upper[:, 16:].T, corner], axis=1)


def call(kernel, shapes, ins, name=None):
    return pl.pallas_call(
        kernel,
        out_shape=[jax.ShapeDtypeStruct(s, F32) for s in shapes],
        in_specs=ins,
        out_specs=[VMEM] * len(shapes),
        compiler_params=pltpu.CompilerParams(vmem_limit_bytes=24 * 1024 * 1024),
        name=name,
    )


def shift(x, axis, size, by):
    return lax.ppermute(x, axis, [(i, (i + by) % size) for i in range(size)])


def chip_groups(slots, mixed):
    order = ORDER_A if mixed else ORDER_C
    return [
        [
            (chip * slots + slot) * 2 + (1 - core if mixed and chip == order[-1] else core)
            for chip in order
        ]
        for slot in range(slots)
        for core in range(2)
    ]


def exchange(x, slots, mixed):
    groups = chip_groups(slots, mixed)
    return lax.all_to_all(x, ("mz", "rt", "samp"), 0, 0, axis_index_groups=groups)


def local(spectra, sample_factor, scan_factor):
    spectra_other = shift(spectra, "samp", 2, 1)
    sample = jnp.pad(sample_factor.T, ((0, 0), (0, 128 - RANK)))
    packet = jnp.concatenate([scan_factor.reshape(4, 128), sample], axis=0)
    gathered = exchange(jnp.broadcast_to(packet[None], (RANK,) + packet.shape), 4, True)
    (partial,) = call(contract_kernel, [(RANK, BINS + 128)], [VMEM] * 2, name="contract")(
        spectra_other, gathered
    )
    far = [shift(partial, "rt", 4, by) for by in (1, 3, 2)]
    mine = (partial + far[2]) + (far[0] + far[1])
    other = shift(mine, "samp", 2, 1)
    (inverse,) = call(invert_kernel, [(RANK, RANK)], [VMEM], name="invert")(mine)
    raw, packets = call(solve_kernel, [(RANK, 64), (RANK, 8, 128)], [VMEM] * 3, name="solve")(
        mine, other, inverse
    )
    packets = exchange(packets, 4, False)
    factor, peak, gram = call(
        finish_kernel, [(RANK, 64), (1, RANK), (RANK, RANK)], [VMEM] * 2, name="finish"
    )(packets, raw)
    return (factor, peak.reshape(RANK), gram)


def solution(mesh):
    return jax.shard_map(
        local,
        mesh=mesh,
        in_specs=(P("samp", "rt", "mz"), P(None, "samp"), P("mz", "rt")),
        out_specs=(P(None, ("mz", "rt", "samp")), P(), P()),
        check_vma=False,
    )
```

```python
import jax
import jax.numpy as jnp
from jax import lax
from jax.experimental import pallas as pl
from jax.experimental.pallas import tpu as pltpu
from jax.sharding import PartitionSpec as P

MZ = 16384
RANK = 32
BINS = 512
TILES = BINS // 128
FIRST = 18
HIGHEST = lax.Precision.HIGHEST
F32 = jnp.float32
BF16 = jnp.bfloat16
VMEM = pl.BlockSpec(memory_space=pltpu.VMEM)


def iota(shape, dim):
    return lax.broadcasted_iota(jnp.int32, shape, dim)


def split(x):
    high = x.astype(BF16)
    return high, (x - high.astype(F32)).astype(BF16)


def dot(a, b):
    return jnp.dot(a, b, precision=HIGHEST, preferred_element_type=F32)


def nt_dot(a, b, precision=HIGHEST):
    return lax.dot_general(
        a, b, (((1,), (1,)), ((), ())), precision=precision, preferred_element_type=F32
    )


def as_column(row):
    n = row.shape[1]
    return jnp.sum(jnp.where(iota((n, n), 0) == iota((n, n), 1), row, 0.0), axis=1, keepdims=True)


def dist(a, b):
    z, y = abs(a // 4 - b // 4), abs(a % 4 - b % 4)
    return min(z, 8 - z) + min(y, 4 - y)


def ordered(key):
    return [FIRST] + sorted([c for c in range(RANK) if c != FIRST], key=key)


ORDER_A = [(FIRST + i) % RANK for i in range(RANK)]
ORDER_C = ordered(lambda chip: dist(chip, 0))


def in_order(x):
    place = [ORDER_A.index(chip) for chip in range(RANK)]
    pieces, start = [], 0
    for i in range(1, RANK + 1):
        if i == RANK or place[i] != place[i - 1] + 1:
            pieces.append(x[place[start] : place[start] + i - start])
            start = i
    return jnp.concatenate(pieces, axis=0) if len(pieces) > 1 else x


def contract_kernel(spectra_ref, gathered_ref, out_ref):
    scan = jnp.concatenate([gathered_ref[:, u, :] for u in range(4)], axis=1)
    scan = in_order(scan)
    scan_high, scan_low = split(scan)
    stacked = jnp.concatenate([scan_high, scan_low], axis=0)
    last = gathered_ref.shape[0] - 1
    swapped = lax.axis_index("mz") == ORDER_A[-1]
    total = jnp.zeros((RANK, BINS), F32)
    gram = jnp.zeros((RANK, RANK), F32)
    for s in range(spectra_ref.shape[0]):
        one, two = (gathered_ref[d, 4 + s : 5 + s, :RANK] for d in (0, last))
        one_column, two_column = as_column(one), as_column(two)
        gram = gram + (one_column * one + two_column * two)
        high, low = split(spectra_ref[s])
        both = jnp.dot(stacked, high, preferred_element_type=F32)
        part = both[:RANK] + both[RANK:] + jnp.dot(scan_high, low, preferred_element_type=F32)
        total = total + jnp.where(swapped, one_column, two_column) * part
    for t in range(TILES):
        out_ref[t * RANK : (t + 1) * RANK] = total[:, t * 128 : (t + 1) * 128]
    system = gram * nt_dot(scan, scan)
    out_ref[TILES * RANK :] = jnp.concatenate([system[8 * t : 8 * t + 8] for t in range(4)], axis=1)


def invert_kernel(total_ref, out_ref):
    system = total_ref[TILES * RANK :]
    tiles = RANK // 8
    columns = [
        [
            jnp.broadcast_to(system[:, RANK * t + j : RANK * t + j + 1], (8, 128))
            for t in range(tiles)
        ]
        for j in range(RANK)
    ]
    row, lane = iota((8, 128), 0), iota((8, 128), 1)
    work = [jnp.where(row + 8 * t == lane, 1.0, 0.0) for t in range(tiles)]
    pivots = [jnp.ones((8, 128), F32)] * tiles
    for k in range(RANK):
        top, r = divmod(k, 8)
        pivot = columns[k][top][r : r + 1]
        pivots[top] = jnp.where(row == r, pivot, pivots[top])
        scale = 1.0 / pivot
        factor = [columns[k][t] * scale if t >= top else None for t in range(tiles)]
        factor[top] = jnp.where(row > r, factor[top], 0.0)
        pivot_row = work[top][r : r + 1]
        for t in range(top, tiles):
            work[t] = work[t] - factor[t] * pivot_row
            for j in range(k + 1, min(8 * t + 8, RANK)):
                other = columns[k][j // 8][j % 8 : j % 8 + 1]
                columns[j][t] = columns[j][t] - factor[t] * other
    factor = jnp.concatenate(
        [(work[t] * lax.rsqrt(pivots[t]))[:, :RANK] for t in range(tiles)], axis=0
    )
    out_ref[...] = dot(factor.T, factor)


def solve_kernel(mine_ref, other_ref, inverse_ref, raw_ref, packet_ref):
    parts = [slice(t * RANK, (t + 1) * RANK) for t in range(TILES)]
    product = jnp.concatenate([mine_ref[part] + other_ref[part] for part in parts], axis=1)
    raw = dot(inverse_ref[...], product)
    slot, core = lax.axis_index("rt"), lax.axis_index("samp")
    tiles = [raw[:, t * 128 : (t + 1) * 128] for t in range(TILES)]
    own = jnp.where(
        slot < 2,
        jnp.where(slot == 0, tiles[0], tiles[1]),
        jnp.where(slot == 2, tiles[2], tiles[3]),
    )
    raw_ref[...] = jnp.where(core == 0, own, pltpu.roll(own, 64, 1))[:, :64]
    peak = jnp.max(jnp.abs(raw), axis=1, keepdims=True) + 1e-06
    high, low = split(raw * (1.0 / peak))
    both = nt_dot(jnp.concatenate([high, low], axis=0), high, None)
    gram = both[:RANK] + both[RANK:] + nt_dot(high, low, None)
    diagonal = iota((RANK, RANK), 0) == iota((RANK, RANK), 1)
    peak_row = jnp.sum(jnp.where(diagonal, peak, 0.0), axis=0, keepdims=True)
    packet = jnp.concatenate(
        [gram[:8], gram[8:16], gram[16:24, 16:], gram[24:, 16:], jnp.broadcast_to(peak_row, (8, RANK))],
        axis=1,
    )
    for d in range(packet_ref.shape[0]):
        packet_ref[d] = packet


def take_lanes(x, lanes):
    return jnp.take_along_axis(x, lanes, axis=1, mode="promise_in_bounds")


def finish_kernel(packets_ref, raw_ref, factor_ref, peak_ref, gram_ref):
    count = packets_ref.shape[0]
    peaks = packets_ref[0]
    for d in range(1, count):
        peaks = jnp.maximum(peaks, packets_ref[d])
    scale = 1.0 / peaks
    row, lane = iota((8, 128), 0), iota((8, 128), 1)
    block = jnp.where(lane < 64, lane >> 5, jnp.where(lane < 80, 2, 3))
    of_row = 96 + 8 * block + row
    of_column = 96 + jnp.where(lane < 64, lane & 31, 16 + (lane & 15))
    total = jnp.zeros((8, 128), F32)
    for d in range(count):
        packet = packets_ref[d]
        ratio = packet * scale
        total = total + packet * take_lanes(ratio, of_row) * take_lanes(ratio, of_column)
    total = total * (1.0 / MZ)
    peak_ref[...] = peaks[:1, 96:]
    for t in range(RANK // 8):
        rows = slice(8 * t, 8 * t + 8)
        factor_ref[rows] = raw_ref[rows] / take_lanes(peaks, 96 + 8 * t + row)[:, :64]
    upper = jnp.concatenate([total[:, :32], total[:, 32:64]], axis=0)
    corner = jnp.concatenate([total[:, 64:80], total[:, 80:96]], axis=0)
    gram_ref[:16] = upper
    gram_ref[16:] = jnp.concatenate([upper[:, 16:].T, corner], axis=1)


def call(kernel, shapes, ins, name=None):
    return pl.pallas_call(
        kernel,
        out_shape=[jax.ShapeDtypeStruct(s, F32) for s in shapes],
        in_specs=ins,
        out_specs=[VMEM] * len(shapes),
        compiler_params=pltpu.CompilerParams(vmem_limit_bytes=24 * 1024 * 1024),
        name=name,
    )


def shift(x, axis, size, by):
    return lax.ppermute(x, axis, [(i, (i + by) % size) for i in range(size)])


def swap(x, slots, core):
    pairs = [(i, i ^ (2 * slots + core)) for i in range(8)]
    return lax.ppermute(x, ("rt", "samp"), pairs)


def chip_groups(slots, mixed):
    order = ORDER_A if mixed else ORDER_C
    return [
        [
            (chip * slots + slot) * 2 + (1 - core if mixed and chip == order[-1] else core)
            for chip in order
        ]
        for slot in range(slots)
        for core in range(2)
    ]


def exchange(x, slots, mixed):
    groups = chip_groups(slots, mixed)
    return lax.all_to_all(x, ("mz", "rt", "samp"), 0, 0, axis_index_groups=groups)


def local(spectra, sample_factor, scan_factor):
    spectra_other = shift(spectra, "samp", 2, 1)
    sample = jnp.pad(sample_factor.T, ((0, 0), (0, 128 - RANK)))
    packet = jnp.concatenate([scan_factor.reshape(4, 128), sample], axis=0)
    gathered = exchange(jnp.broadcast_to(packet[None], (RANK,) + packet.shape), 4, True)
    (partial,) = call(contract_kernel, [(TILES * RANK + 8, 128)], [VMEM] * 2, name="contract")(
        spectra_other, gathered
    )
    two, three, one = (swap(partial, slots, core) for slots, core in ((2, 1), (3, 0), (1, 1)))
    mine = (partial + one) + (two + three)
    other = shift(mine, "samp", 2, 1)
    (inverse,) = call(invert_kernel, [(RANK, RANK)], [VMEM], name="invert")(mine)
    raw, packets = call(solve_kernel, [(RANK, 64), (RANK, 8, 128)], [VMEM] * 3, name="solve")(
        mine, other, inverse
    )
    packets = exchange(packets, 4, False)
    factor, peak, gram = call(
        finish_kernel, [(RANK, 64), (1, RANK), (RANK, RANK)], [VMEM] * 2, name="finish"
    )(packets, raw)
    return (factor, peak.reshape(RANK), gram)


def solution(mesh):
    return jax.shard_map(
        local,
        mesh=mesh,
        in_specs=(P("samp", "rt", "mz"), P(None, "samp"), P("mz", "rt")),
        out_specs=(P(None, ("mz", "rt", "samp")), P(), P()),
        check_vma=False,
    )
```

```python
import jax
import jax.numpy as jnp
from jax import lax
from jax.experimental import pallas as pl
from jax.experimental.pallas import tpu as pltpu
from jax.sharding import PartitionSpec as P

MZ = 16384
RANK = 32
BINS = 512
TILES = BINS // 128
FIRST = 18
HIGHEST = lax.Precision.HIGHEST
F32 = jnp.float32
BF16 = jnp.bfloat16
VMEM = pl.BlockSpec(memory_space=pltpu.VMEM)


def iota(shape, dim):
    return lax.broadcasted_iota(jnp.int32, shape, dim)


def split(x):
    high = x.astype(BF16)
    return high, (x - high.astype(F32)).astype(BF16)


def dot(a, b):
    return jnp.dot(a, b, precision=HIGHEST, preferred_element_type=F32)


def nt_dot(a, b, precision=HIGHEST):
    return lax.dot_general(
        a, b, (((1,), (1,)), ((), ())), precision=precision, preferred_element_type=F32
    )


def as_column(row):
    n = row.shape[1]
    return jnp.sum(jnp.where(iota((n, n), 0) == iota((n, n), 1), row, 0.0), axis=1, keepdims=True)


def dist(a, b):
    z, y = abs(a // 4 - b // 4), abs(a % 4 - b % 4)
    return min(z, 8 - z) + min(y, 4 - y)


def ordered(key):
    return [FIRST] + sorted([c for c in range(RANK) if c != FIRST], key=key)


ORDER_A = [(FIRST + i) % RANK for i in range(RANK)]
ORDER_C = ordered(lambda chip: dist(chip, 0))


def in_order(x):
    place = [ORDER_A.index(chip) for chip in range(RANK)]
    pieces, start = [], 0
    for i in range(1, RANK + 1):
        if i == RANK or place[i] != place[i - 1] + 1:
            pieces.append(x[place[start] : place[start] + i - start])
            start = i
    return jnp.concatenate(pieces, axis=0) if len(pieces) > 1 else x


def spread_kernel(packet_ref, out_ref):
    pieces = [packet_ref[u : u + 1] for u in range(4)]
    pieces += [packet_ref[4 + s : 5 + s, :RANK] for s in range(4)]
    row = jnp.concatenate(pieces, axis=1)
    for d in range(out_ref.shape[0]):
        out_ref[d] = row


def contract_kernel(spectra_ref, gathered_ref, out_ref):
    scan = gathered_ref[:, :BINS]
    scan = in_order(scan)
    scan_high, scan_low = split(scan)
    stacked = jnp.concatenate([scan_high, scan_low], axis=0)
    last = gathered_ref.shape[0] - 1
    swapped = lax.axis_index("mz") == ORDER_A[-1]
    total = jnp.zeros((RANK, BINS), F32)
    gram = jnp.zeros((RANK, RANK), F32)
    for s in range(spectra_ref.shape[0]):
        one, two = (gathered_ref[d : d + 1, BINS + s * RANK : BINS + (s + 1) * RANK] for d in (0, last))
        one_column, two_column = as_column(one), as_column(two)
        gram = gram + (one_column * one + two_column * two)
        high, low = split(spectra_ref[s])
        both = jnp.dot(stacked, high, preferred_element_type=F32)
        part = both[:RANK] + both[RANK:] + jnp.dot(scan_high, low, preferred_element_type=F32)
        total = total + jnp.where(swapped, one_column, two_column) * part
    for t in range(TILES):
        out_ref[t * RANK : (t + 1) * RANK] = total[:, t * 128 : (t + 1) * 128]
    system = gram * nt_dot(scan, scan)
    out_ref[TILES * RANK :] = jnp.concatenate([system[8 * t : 8 * t + 8] for t in range(4)], axis=1)


def invert_kernel(total_ref, out_ref):
    system = total_ref[TILES * RANK :]
    tiles = RANK // 8
    columns = [
        [
            jnp.broadcast_to(system[:, RANK * t + j : RANK * t + j + 1], (8, 128))
            for t in range(tiles)
        ]
        for j in range(RANK)
    ]
    row, lane = iota((8, 128), 0), iota((8, 128), 1)
    work = [jnp.where(row + 8 * t == lane, 1.0, 0.0) for t in range(tiles)]
    pivots = [jnp.ones((8, 128), F32)] * tiles
    for k in range(RANK):
        top, r = divmod(k, 8)
        pivot = columns[k][top][r : r + 1]
        pivots[top] = jnp.where(row == r, pivot, pivots[top])
        scale = 1.0 / pivot
        factor = [columns[k][t] * scale if t >= top else None for t in range(tiles)]
        factor[top] = jnp.where(row > r, factor[top], 0.0)
        pivot_row = work[top][r : r + 1]
        for t in range(top, tiles):
            work[t] = work[t] - factor[t] * pivot_row
            for j in range(k + 1, min(8 * t + 8, RANK)):
                other = columns[k][j // 8][j % 8 : j % 8 + 1]
                columns[j][t] = columns[j][t] - factor[t] * other
    factor = jnp.concatenate(
        [(work[t] * lax.rsqrt(pivots[t]))[:, :RANK] for t in range(tiles)], axis=0
    )
    out_ref[...] = dot(factor.T, factor)


def solve_kernel(mine_ref, other_ref, inverse_ref, raw_ref, packet_ref):
    parts = [slice(t * RANK, (t + 1) * RANK) for t in range(TILES)]
    product = jnp.concatenate([mine_ref[part] + other_ref[part] for part in parts], axis=1)
    raw = dot(inverse_ref[...], product)
    slot, core = lax.axis_index("rt"), lax.axis_index("samp")
    tiles = [raw[:, t * 128 : (t + 1) * 128] for t in range(TILES)]
    own = jnp.where(
        slot < 2,
        jnp.where(slot == 0, tiles[0], tiles[1]),
        jnp.where(slot == 2, tiles[2], tiles[3]),
    )
    raw_ref[...] = jnp.where(core == 0, own, pltpu.roll(own, 64, 1))[:, :64]
    peak = jnp.max(jnp.abs(raw), axis=1, keepdims=True) + 1e-06
    high, low = split(raw * (1.0 / peak))
    both = nt_dot(jnp.concatenate([high, low], axis=0), high, None)
    gram = both[:RANK] + both[RANK:] + nt_dot(high, low, None)
    diagonal = iota((RANK, RANK), 0) == iota((RANK, RANK), 1)
    peak_row = jnp.sum(jnp.where(diagonal, peak, 0.0), axis=0, keepdims=True)
    packet = jnp.concatenate(
        [gram[:8], gram[8:16], gram[16:24, 16:], gram[24:, 16:], jnp.broadcast_to(peak_row, (8, RANK))],
        axis=1,
    )
    for d in range(packet_ref.shape[0]):
        packet_ref[d] = packet


def take_lanes(x, lanes):
    return jnp.take_along_axis(x, lanes, axis=1, mode="promise_in_bounds")


def finish_kernel(packets_ref, raw_ref, factor_ref, peak_ref, gram_ref):
    count = packets_ref.shape[0]
    peaks = packets_ref[0]
    for d in range(1, count):
        peaks = jnp.maximum(peaks, packets_ref[d])
    scale = 1.0 / peaks
    row, lane = iota((8, 128), 0), iota((8, 128), 1)
    block = jnp.where(lane < 64, lane >> 5, jnp.where(lane < 80, 2, 3))
    of_row = 96 + 8 * block + row
    of_column = 96 + jnp.where(lane < 64, lane & 31, 16 + (lane & 15))
    total = jnp.zeros((8, 128), F32)
    for d in range(count):
        packet = packets_ref[d]
        ratio = packet * scale
        total = total + packet * take_lanes(ratio, of_row) * take_lanes(ratio, of_column)
    total = total * (1.0 / MZ)
    peak_ref[...] = peaks[:1, 96:]
    for t in range(RANK // 8):
        rows = slice(8 * t, 8 * t + 8)
        factor_ref[rows] = raw_ref[rows] / take_lanes(peaks, 96 + 8 * t + row)[:, :64]
    upper = jnp.concatenate([total[:, :32], total[:, 32:64]], axis=0)
    corner = jnp.concatenate([total[:, 64:80], total[:, 80:96]], axis=0)
    gram_ref[:16] = upper
    gram_ref[16:] = jnp.concatenate([upper[:, 16:].T, corner], axis=1)


def call(kernel, shapes, ins, name=None):
    return pl.pallas_call(
        kernel,
        out_shape=[jax.ShapeDtypeStruct(s, F32) for s in shapes],
        in_specs=ins,
        out_specs=[VMEM] * len(shapes),
        compiler_params=pltpu.CompilerParams(vmem_limit_bytes=24 * 1024 * 1024),
        name=name,
    )


def shift(x, axis, size, by):
    return lax.ppermute(x, axis, [(i, (i + by) % size) for i in range(size)])


def swap(x, slots, core):
    pairs = [(i, i ^ (2 * slots + core)) for i in range(8)]
    return lax.ppermute(x, ("rt", "samp"), pairs)


def chip_groups(slots, mixed):
    order = ORDER_A if mixed else ORDER_C
    return [
        [
            (chip * slots + slot) * 2 + (1 - core if mixed and chip == order[-1] else core)
            for chip in order
        ]
        for slot in range(slots)
        for core in range(2)
    ]


def exchange(x, slots, mixed):
    groups = chip_groups(slots, mixed)
    return lax.all_to_all(x, ("mz", "rt", "samp"), 0, 0, axis_index_groups=groups)


def local(spectra, sample_factor, scan_factor):
    spectra_other = shift(spectra, "samp", 2, 1)
    sample = jnp.pad(sample_factor.T, ((0, 0), (0, 128 - RANK)))
    packet = jnp.concatenate([scan_factor.reshape(4, 128), sample], axis=0)
    width = BINS + 128
    (packets,) = call(spread_kernel, [(RANK, 1, width)], [VMEM], name="spread")(packet)
    gathered = exchange(packets, 4, True).reshape(RANK, width)
    (partial,) = call(contract_kernel, [(TILES * RANK + 8, 128)], [VMEM] * 2, name="contract")(
        spectra_other, gathered
    )
    two, three, one = (swap(partial, slots, core) for slots, core in ((2, 1), (3, 0), (1, 1)))
    mine = (partial + one) + (two + three)
    other = shift(mine, "samp", 2, 1)
    (inverse,) = call(invert_kernel, [(RANK, RANK)], [VMEM], name="invert")(mine)
    raw, packets = call(solve_kernel, [(RANK, 64), (RANK, 8, 128)], [VMEM] * 3, name="solve")(
        mine, other, inverse
    )
    packets = exchange(packets, 4, False)
    factor, peak, gram = call(
        finish_kernel, [(RANK, 64), (1, RANK), (RANK, RANK)], [VMEM] * 2, name="finish"
    )(packets, raw)
    return (factor, peak.reshape(RANK), gram)


def solution(mesh):
    return jax.shard_map(
        local,
        mesh=mesh,
        in_specs=(P("samp", "rt", "mz"), P(None, "samp"), P("mz", "rt")),
        out_specs=(P(None, ("mz", "rt", "samp")), P(), P()),
        check_vma=False,
    )
```

```python
import jax
import jax.numpy as jnp
from jax import lax
from jax.experimental import pallas as pl
from jax.experimental.pallas import tpu as pltpu
from jax.sharding import PartitionSpec as P

MZ = 16384
RANK = 32
BINS = 512
TILES = BINS // 128
FIRST = 18
HIGHEST = lax.Precision.HIGHEST
F32 = jnp.float32
BF16 = jnp.bfloat16
VMEM = pl.BlockSpec(memory_space=pltpu.VMEM)


def iota(shape, dim):
    return lax.broadcasted_iota(jnp.int32, shape, dim)


def split(x):
    high = x.astype(BF16)
    return high, (x - high.astype(F32)).astype(BF16)


def dot(a, b):
    return jnp.dot(a, b, precision=HIGHEST, preferred_element_type=F32)


def nt_dot(a, b, precision=HIGHEST):
    return lax.dot_general(
        a, b, (((1,), (1,)), ((), ())), precision=precision, preferred_element_type=F32
    )


def as_column(row):
    n = row.shape[1]
    return jnp.sum(jnp.where(iota((n, n), 0) == iota((n, n), 1), row, 0.0), axis=1, keepdims=True)


def dist(a, b):
    z, y = abs(a // 4 - b // 4), abs(a % 4 - b % 4)
    return min(z, 8 - z) + min(y, 4 - y)


def ordered(key):
    return [FIRST] + sorted([c for c in range(RANK) if c != FIRST], key=key)


ORDER_A = [(FIRST + i) % RANK for i in range(RANK)]
ORDER_C = ordered(lambda chip: dist(chip, 0))


def in_order(x):
    place = [ORDER_A.index(chip) for chip in range(RANK)]
    pieces, start = [], 0
    for i in range(1, RANK + 1):
        if i == RANK or place[i] != place[i - 1] + 1:
            pieces.append(x[place[start] : place[start] + i - start])
            start = i
    return jnp.concatenate(pieces, axis=0) if len(pieces) > 1 else x


def spread_kernel(packet_ref, out_ref):
    pieces = [packet_ref[u : u + 1] for u in range(4)]
    pieces += [packet_ref[4 + s : 5 + s, :RANK] for s in range(4)]
    row = jnp.concatenate(pieces, axis=1)
    for d in range(out_ref.shape[0]):
        out_ref[d] = row


def contract_kernel(spectra_ref, gathered_ref, out_ref):
    scan = gathered_ref[:, :BINS]
    scan = in_order(scan)
    scan_high, scan_low = split(scan)
    stacked = jnp.concatenate([scan_high, scan_low], axis=0)
    last = gathered_ref.shape[0] - 1
    swapped = lax.axis_index("mz") == ORDER_A[-1]
    total = jnp.zeros((RANK, BINS), F32)
    gram = jnp.zeros((RANK, RANK), F32)
    for s in range(spectra_ref.shape[0]):
        one, two = (gathered_ref[d : d + 1, BINS + s * RANK : BINS + (s + 1) * RANK] for d in (0, last))
        one_column, two_column = as_column(one), as_column(two)
        gram = gram + (one_column * one + two_column * two)
        high, low = split(spectra_ref[s])
        both = jnp.dot(stacked, high, preferred_element_type=F32)
        part = both[:RANK] + both[RANK:] + jnp.dot(scan_high, low, preferred_element_type=F32)
        total = total + jnp.where(swapped, one_column, two_column) * part
    for t in range(TILES):
        out_ref[t * RANK : (t + 1) * RANK] = total[:, t * 128 : (t + 1) * 128]
    system = gram * nt_dot(scan, scan)
    out_ref[TILES * RANK :] = jnp.concatenate([system[8 * t : 8 * t + 8] for t in range(4)], axis=1)


def invert_kernel(total_ref, out_ref):
    system = total_ref[TILES * RANK :]
    tiles = RANK // 8
    columns = [
        [
            jnp.broadcast_to(system[:, RANK * t + j : RANK * t + j + 1], (8, 128))
            for t in range(tiles)
        ]
        for j in range(RANK)
    ]
    row, lane = iota((8, 128), 0), iota((8, 128), 1)
    work = [jnp.where(row + 8 * t == lane, 1.0, 0.0) for t in range(tiles)]
    pivots = [jnp.ones((8, 128), F32)] * tiles
    for k in range(RANK):
        top, r = divmod(k, 8)
        pivot = columns[k][top][r : r + 1]
        pivots[top] = jnp.where(row == r, pivot, pivots[top])
        scale = 1.0 / pivot
        factor = [columns[k][t] * scale if t >= top else None for t in range(tiles)]
        factor[top] = jnp.where(row > r, factor[top], 0.0)
        pivot_row = work[top][r : r + 1]
        for t in range(top, tiles):
            work[t] = work[t] - factor[t] * pivot_row
            for j in range(k + 1, min(8 * t + 8, RANK)):
                other = columns[k][j // 8][j % 8 : j % 8 + 1]
                columns[j][t] = columns[j][t] - factor[t] * other
    factor = jnp.concatenate(
        [(work[t] * lax.rsqrt(pivots[t]))[:, :RANK] for t in range(tiles)], axis=0
    )
    out_ref[...] = dot(factor.T, factor)


def solve_kernel(mine_ref, other_ref, inverse_ref, raw_ref, packet_ref):
    parts = [slice(t * RANK, (t + 1) * RANK) for t in range(TILES)]
    product = jnp.concatenate([mine_ref[part] + other_ref[part] for part in parts], axis=1)
    raw = dot(inverse_ref[...], product)
    slot, core = lax.axis_index("rt"), lax.axis_index("samp")
    tiles = [raw[:, t * 128 : (t + 1) * 128] for t in range(TILES)]
    own = jnp.where(
        slot < 2,
        jnp.where(slot == 0, tiles[0], tiles[1]),
        jnp.where(slot == 2, tiles[2], tiles[3]),
    )
    raw_ref[...] = jnp.where(core == 0, own, pltpu.roll(own, 64, 1))[:, :64]
    peak = jnp.max(jnp.abs(raw), axis=1, keepdims=True) + 1e-06
    high, low = split(raw * (1.0 / peak))
    both = nt_dot(jnp.concatenate([high, low], axis=0), high, None)
    gram = both[:RANK] + both[RANK:] + nt_dot(high, low, None)
    diagonal = iota((RANK, RANK), 0) == iota((RANK, RANK), 1)
    peak_row = jnp.sum(jnp.where(diagonal, peak, 0.0), axis=0, keepdims=True)
    blocks = jnp.concatenate([gram[8 * t : 8 * t + 8, 8 * t :] for t in range(4)], axis=1)
    packet = jnp.concatenate(
        [blocks[u : u + 1] for u in range(8)] + [peak_row, jnp.zeros((1, 96), F32)], axis=1
    )
    for d in range(packet_ref.shape[0]):
        packet_ref[d] = packet


def take_lanes(x, lanes):
    return jnp.take_along_axis(x, lanes, axis=1, mode="promise_in_bounds")


def finish_kernel(packets_ref, raw_ref, factor_ref, peak_ref, gram_ref):
    width = 80
    last = packets_ref[:, 8 * width :]
    peak_row = jnp.max(last, axis=0, keepdims=True)
    ratio = last / peak_row
    tiles = []
    for t in range(5):
        place = iota((8, 128), 1) + 128 * t
        u, lane = place // width, place % width
        block = jnp.where(lane < 32, 0, jnp.where(lane < 56, 1, jnp.where(lane < 72, 2, 3)))
        column = jnp.where(
            lane < 32, lane, jnp.where(lane < 56, lane - 24, jnp.where(lane < 72, lane - 40, lane - 48))
        )
        total = jnp.zeros((8, 128), F32)
        for d in range(0, packets_ref.shape[0], 8):
            scale = ratio[d : d + 8]
            packet = packets_ref[d : d + 8, 128 * t : 128 * t + 128]
            total = total + packet * take_lanes(scale, 8 * block + u) * take_lanes(scale, column)
        tiles.append(jnp.sum(total, axis=0, keepdims=True))
    flat = jnp.concatenate(tiles, axis=1) * (1.0 / MZ)
    blocks = jnp.concatenate([flat[:, width * u : width * (u + 1)] for u in range(8)], axis=0)
    upper = jnp.concatenate(
        [
            blocks[:, :32],
            jnp.concatenate([jnp.zeros((8, 8), F32), blocks[:, 32:56]], axis=1),
            jnp.concatenate([jnp.zeros((8, 16), F32), blocks[:, 56:72]], axis=1),
            jnp.concatenate([jnp.zeros((8, 24), F32), blocks[:, 72:80]], axis=1),
        ],
        axis=0,
    )
    row, column = iota((RANK, RANK), 0), iota((RANK, RANK), 1)
    gram_ref[...] = jnp.where((row >> 3) <= (column >> 3), upper, upper.T)
    peak_ref[...] = peak_row[:, :RANK]
    factor_ref[...] = raw_ref[...] / as_column(peak_row[:, :RANK])


def call(kernel, shapes, ins, name=None):
    return pl.pallas_call(
        kernel,
        out_shape=[jax.ShapeDtypeStruct(s, F32) for s in shapes],
        in_specs=ins,
        out_specs=[VMEM] * len(shapes),
        compiler_params=pltpu.CompilerParams(vmem_limit_bytes=24 * 1024 * 1024),
        name=name,
    )


def shift(x, axis, size, by):
    return lax.ppermute(x, axis, [(i, (i + by) % size) for i in range(size)])


def swap(x, slots, core):
    pairs = [(i, i ^ (2 * slots + core)) for i in range(8)]
    return lax.ppermute(x, ("rt", "samp"), pairs)


def chip_groups(slots, mixed):
    order = ORDER_A if mixed else ORDER_C
    return [
        [
            (chip * slots + slot) * 2 + (1 - core if mixed and chip == order[-1] else core)
            for chip in order
        ]
        for slot in range(slots)
        for core in range(2)
    ]


def exchange(x, slots, mixed):
    groups = chip_groups(slots, mixed)
    return lax.all_to_all(x, ("mz", "rt", "samp"), 0, 0, axis_index_groups=groups)


def local(spectra, sample_factor, scan_factor):
    spectra_other = shift(spectra, "samp", 2, 1)
    sample = jnp.pad(sample_factor.T, ((0, 0), (0, 128 - RANK)))
    packet = jnp.concatenate([scan_factor.reshape(4, 128), sample], axis=0)
    width = BINS + 128
    (packets,) = call(spread_kernel, [(RANK, 1, width)], [VMEM], name="spread")(packet)
    gathered = exchange(packets, 4, True).reshape(RANK, width)
    (partial,) = call(contract_kernel, [(TILES * RANK + 8, 128)], [VMEM] * 2, name="contract")(
        spectra_other, gathered
    )
    two, three, one = (swap(partial, slots, core) for slots, core in ((2, 1), (3, 0), (1, 1)))
    mine = (partial + one) + (two + three)
    other = shift(mine, "samp", 2, 1)
    (inverse,) = call(invert_kernel, [(RANK, RANK)], [VMEM], name="invert")(mine)
    raw, packets = call(solve_kernel, [(RANK, 64), (RANK, 1, 768)], [VMEM] * 3, name="solve")(
        mine, other, inverse
    )
    packets = exchange(packets, 4, False).reshape(RANK, 768)
    factor, peak, gram = call(
        finish_kernel, [(RANK, 64), (1, RANK), (RANK, RANK)], [VMEM] * 2, name="finish"
    )(packets, raw)
    return (factor, peak.reshape(RANK), gram)


def solution(mesh):
    return jax.shard_map(
        local,
        mesh=mesh,
        in_specs=(P("samp", "rt", "mz"), P(None, "samp"), P("mz", "rt")),
        out_specs=(P(None, ("mz", "rt", "samp")), P(), P()),
        check_vma=False,
    )
```

```python
import jax
import jax.numpy as jnp
from jax import lax
from jax.experimental import pallas as pl
from jax.experimental.pallas import tpu as pltpu
from jax.sharding import PartitionSpec as P

MZ = 16384
RANK = 32
BINS = 512
TILES = BINS // 128
FIRST = 18
HIGHEST = lax.Precision.HIGHEST
F32 = jnp.float32
BF16 = jnp.bfloat16
VMEM = pl.BlockSpec(memory_space=pltpu.VMEM)


def iota(shape, dim):
    return lax.broadcasted_iota(jnp.int32, shape, dim)


def split(x):
    high = x.astype(BF16)
    return high, (x - high.astype(F32)).astype(BF16)


def dot(a, b):
    return jnp.dot(a, b, precision=HIGHEST, preferred_element_type=F32)


def nt_dot(a, b, precision=HIGHEST):
    return lax.dot_general(
        a, b, (((1,), (1,)), ((), ())), precision=precision, preferred_element_type=F32
    )


def as_column(row):
    n = row.shape[1]
    return jnp.sum(jnp.where(iota((n, n), 0) == iota((n, n), 1), row, 0.0), axis=1, keepdims=True)


def dist(a, b):
    z, y = abs(a // 4 - b // 4), abs(a % 4 - b % 4)
    return min(z, 8 - z) + min(y, 4 - y)


def ordered(key):
    return [FIRST] + sorted([c for c in range(RANK) if c != FIRST], key=key)


ORDER_A = [(FIRST + i) % RANK for i in range(RANK)]
ORDER_C = ordered(lambda chip: dist(chip, 0))


def in_order(x):
    place = [ORDER_A.index(chip) for chip in range(RANK)]
    pieces, start = [], 0
    for i in range(1, RANK + 1):
        if i == RANK or place[i] != place[i - 1] + 1:
            pieces.append(x[place[start] : place[start] + i - start])
            start = i
    return jnp.concatenate(pieces, axis=0) if len(pieces) > 1 else x


def spread_kernel(packet_ref, out_ref):
    pieces = [packet_ref[u : u + 1] for u in range(4)]
    pieces += [packet_ref[4 + s : 5 + s, :RANK] for s in range(4)]
    row = jnp.concatenate(pieces, axis=1)
    for d in range(out_ref.shape[0]):
        out_ref[d] = row


def contract_kernel(spectra_ref, gathered_ref, out_ref):
    scan = gathered_ref[:, :BINS]
    scan = in_order(scan)
    scan_high, scan_low = split(scan)
    stacked = jnp.concatenate([scan_high, scan_low], axis=0)
    last = gathered_ref.shape[0] - 1
    swapped = lax.axis_index("mz") == ORDER_A[-1]
    total = jnp.zeros((RANK, BINS), F32)
    gram = jnp.zeros((RANK, RANK), F32)
    for s in range(spectra_ref.shape[0]):
        one, two = (gathered_ref[d : d + 1, BINS + s * RANK : BINS + (s + 1) * RANK] for d in (0, last))
        one_column, two_column = as_column(one), as_column(two)
        gram = gram + (one_column * one + two_column * two)
        high, low = split(spectra_ref[s])
        both = jnp.dot(stacked, high, preferred_element_type=F32)
        part = both[:RANK] + both[RANK:] + jnp.dot(scan_high, low, preferred_element_type=F32)
        total = total + jnp.where(swapped, one_column, two_column) * part
    for t in range(TILES):
        out_ref[t * RANK : (t + 1) * RANK] = total[:, t * 128 : (t + 1) * 128]
    system = gram * nt_dot(scan, scan)
    out_ref[TILES * RANK :] = jnp.concatenate([system[8 * t : 8 * t + 8] for t in range(4)], axis=1)


def invert_kernel(total_ref, out_ref):
    system = total_ref[TILES * RANK :]
    tiles = RANK // 8
    columns = [
        [
            jnp.broadcast_to(system[:, RANK * t + j : RANK * t + j + 1], (8, 128))
            for t in range(tiles)
        ]
        for j in range(RANK)
    ]
    row, lane = iota((8, 128), 0), iota((8, 128), 1)
    work = [jnp.where(row + 8 * t == lane, 1.0, 0.0) for t in range(tiles)]
    pivots = [jnp.ones((8, 128), F32)] * tiles
    for k in range(RANK):
        top, r = divmod(k, 8)
        pivot = columns[k][top][r : r + 1]
        pivots[top] = jnp.where(row == r, pivot, pivots[top])
        scale = 1.0 / pivot
        factor = [columns[k][t] * scale if t >= top else None for t in range(tiles)]
        factor[top] = jnp.where(row > r, factor[top], 0.0)
        pivot_row = work[top][r : r + 1]
        for t in range(top, tiles):
            work[t] = work[t] - factor[t] * pivot_row
            for j in range(k + 1, min(8 * t + 8, RANK)):
                other = columns[k][j // 8][j % 8 : j % 8 + 1]
                columns[j][t] = columns[j][t] - factor[t] * other
    factor = jnp.concatenate(
        [(work[t] * lax.rsqrt(pivots[t]))[:, :RANK] for t in range(tiles)], axis=0
    )
    out_ref[...] = dot(factor.T, factor)


def solve_kernel(mine_ref, other_ref, inverse_ref, raw_ref, packet_ref):
    parts = [slice(t * RANK, (t + 1) * RANK) for t in range(TILES)]
    product = jnp.concatenate([mine_ref[part] + other_ref[part] for part in parts], axis=1)
    raw = dot(inverse_ref[...], product)
    slot, core = lax.axis_index("rt"), lax.axis_index("samp")
    tiles = [raw[:, t * 128 : (t + 1) * 128] for t in range(TILES)]
    own = jnp.where(
        slot < 2,
        jnp.where(slot == 0, tiles[0], tiles[1]),
        jnp.where(slot == 2, tiles[2], tiles[3]),
    )
    raw_ref[...] = jnp.where(core == 0, own, pltpu.roll(own, 64, 1))[:, :64]
    peak = jnp.max(jnp.abs(raw), axis=1, keepdims=True) + 1e-06
    high, low = split(raw * (1.0 / peak))
    both = nt_dot(jnp.concatenate([high, low], axis=0), high, None)
    gram = both[:RANK] + both[RANK:] + nt_dot(high, low, None)
    diagonal = iota((RANK, RANK), 0) == iota((RANK, RANK), 1)
    peak_row = jnp.sum(jnp.where(diagonal, peak, 0.0), axis=0, keepdims=True)
    row, column = iota((RANK, RANK), 0), iota((RANK, RANK), 1)
    within = (row >> 3) == (column >> 3)
    turned = jnp.concatenate([peak_row[:, 7:], peak_row[:, :7]], axis=1)
    gram = jnp.where(within & ((row & 7) == 7) & ((column & 7) < 7), peak_row, gram)
    gram = jnp.where(within & ((row & 7) == 6) & ((column & 7) == 0), turned, gram)
    blocks = jnp.concatenate([gram[8 * t : 8 * t + 8, 8 * t :] for t in range(4)], axis=1)
    packet = jnp.concatenate([blocks[u : u + 1] for u in range(8)], axis=1)
    for d in range(packet_ref.shape[0]):
        packet_ref[d] = packet


def take_lanes(x, lanes):
    return jnp.take_along_axis(x, lanes, axis=1, mode="promise_in_bounds")


def finish_kernel(packets_ref, raw_ref, factor_ref, peak_ref, gram_ref):
    width = 80
    component = iota((8, 128), 1) & (RANK - 1)
    offset = jnp.where(component < 8, 0, jnp.where(component < 16, 32, jnp.where(component < 24, 56, 72)))
    eighth = (component & 7) == 7
    place = jnp.where(eighth, jnp.maximum(offset - 32, 0), 48 + offset + (component & 7))
    peaks = []
    for d in range(0, packets_ref.shape[0], 8):
        first = take_lanes(packets_ref[d : d + 8, 384:512], jnp.full((8, 128), 96, jnp.int32))
        rest = take_lanes(packets_ref[d : d + 8, 512:], place)
        peaks.append(jnp.where(component == 7, first, rest))
    peaks = jnp.concatenate(peaks, axis=0)
    peak_row = jnp.max(peaks, axis=0, keepdims=True)
    ratio = peaks / peak_row
    tiles = []
    for t in range(5):
        place = iota((8, 128), 1) + 128 * t
        u, lane = place // width, place % width
        block = jnp.where(lane < 32, 0, jnp.where(lane < 56, 1, jnp.where(lane < 72, 2, 3)))
        column = jnp.where(
            lane < 32, lane, jnp.where(lane < 56, lane - 24, jnp.where(lane < 72, lane - 40, lane - 48))
        )
        total = jnp.zeros((8, 128), F32)
        for d in range(0, packets_ref.shape[0], 8):
            scale = ratio[d : d + 8]
            packet = packets_ref[d : d + 8, 128 * t : 128 * t + 128]
            total = total + packet * take_lanes(scale, 8 * block + u) * take_lanes(scale, column)
        tiles.append(jnp.sum(total, axis=0, keepdims=True))
    flat = jnp.concatenate(tiles, axis=1) * (1.0 / MZ)
    blocks = jnp.concatenate([flat[:, width * u : width * (u + 1)] for u in range(8)], axis=0)
    upper = jnp.concatenate(
        [
            blocks[:, :32],
            jnp.concatenate([jnp.zeros((8, 8), F32), blocks[:, 32:56]], axis=1),
            jnp.concatenate([jnp.zeros((8, 16), F32), blocks[:, 56:72]], axis=1),
            jnp.concatenate([jnp.zeros((8, 24), F32), blocks[:, 72:80]], axis=1),
        ],
        axis=0,
    )
    row, column = iota((RANK, RANK), 0), iota((RANK, RANK), 1)
    gram_ref[...] = jnp.where(row <= column, upper, upper.T)
    peak_ref[...] = peak_row[:, :RANK]
    factor_ref[...] = raw_ref[...] / as_column(peak_row[:, :RANK])


def call(kernel, shapes, ins, name=None):
    return pl.pallas_call(
        kernel,
        out_shape=[jax.ShapeDtypeStruct(s, F32) for s in shapes],
        in_specs=ins,
        out_specs=[VMEM] * len(shapes),
        compiler_params=pltpu.CompilerParams(vmem_limit_bytes=24 * 1024 * 1024),
        name=name,
    )


def shift(x, axis, size, by):
    return lax.ppermute(x, axis, [(i, (i + by) % size) for i in range(size)])


def swap(x, slots, core):
    pairs = [(i, i ^ (2 * slots + core)) for i in range(8)]
    return lax.ppermute(x, ("rt", "samp"), pairs)


def chip_groups(slots, mixed):
    order = ORDER_A if mixed else ORDER_C
    return [
        [
            (chip * slots + slot) * 2 + (1 - core if mixed and chip == order[-1] else core)
            for chip in order
        ]
        for slot in range(slots)
        for core in range(2)
    ]


def exchange(x, slots, mixed):
    groups = chip_groups(slots, mixed)
    return lax.all_to_all(x, ("mz", "rt", "samp"), 0, 0, axis_index_groups=groups)


def local(spectra, sample_factor, scan_factor):
    spectra_other = shift(spectra, "samp", 2, 1)
    sample = jnp.pad(sample_factor.T, ((0, 0), (0, 128 - RANK)))
    packet = jnp.concatenate([scan_factor.reshape(4, 128), sample], axis=0)
    width = BINS + 128
    (packets,) = call(spread_kernel, [(RANK, 1, width)], [VMEM], name="spread")(packet)
    gathered = exchange(packets, 4, True).reshape(RANK, width)
    (partial,) = call(contract_kernel, [(TILES * RANK + 8, 128)], [VMEM] * 2, name="contract")(
        spectra_other, gathered
    )
    two, three, one = (swap(partial, slots, core) for slots, core in ((2, 1), (3, 0), (1, 1)))
    mine = (partial + one) + (two + three)
    other = shift(mine, "samp", 2, 1)
    (inverse,) = call(invert_kernel, [(RANK, RANK)], [VMEM], name="invert")(mine)
    raw, packets = call(solve_kernel, [(RANK, 64), (RANK, 1, 640)], [VMEM] * 3, name="solve")(
        mine, other, inverse
    )
    packets = exchange(packets, 4, False).reshape(RANK, 640)
    factor, peak, gram = call(
        finish_kernel, [(RANK, 64), (1, RANK), (RANK, RANK)], [VMEM] * 2, name="finish"
    )(packets, raw)
    return (factor, peak.reshape(RANK), gram)


def solution(mesh):
    return jax.shard_map(
        local,
        mesh=mesh,
        in_specs=(P("samp", "rt", "mz"), P(None, "samp"), P("mz", "rt")),
        out_specs=(P(None, ("mz", "rt", "samp")), P(), P()),
        check_vma=False,
    )
```

```python
import jax
import jax.numpy as jnp
from jax import lax
from jax.experimental import pallas as pl
from jax.experimental.pallas import tpu as pltpu
from jax.sharding import PartitionSpec as P

MZ = 16384
RANK = 32
BINS = 512
TILES = BINS // 128
FIRST = 18
HIGHEST = lax.Precision.HIGHEST
F32 = jnp.float32
BF16 = jnp.bfloat16
VMEM = pl.BlockSpec(memory_space=pltpu.VMEM)


def iota(shape, dim):
    return lax.broadcasted_iota(jnp.int32, shape, dim)


def split(x):
    high = x.astype(BF16)
    return high, (x - high.astype(F32)).astype(BF16)


def dot(a, b):
    return jnp.dot(a, b, precision=HIGHEST, preferred_element_type=F32)


def nt_dot(a, b, precision=HIGHEST):
    return lax.dot_general(
        a, b, (((1,), (1,)), ((), ())), precision=precision, preferred_element_type=F32
    )


def as_column(row):
    n = row.shape[1]
    return jnp.sum(jnp.where(iota((n, n), 0) == iota((n, n), 1), row, 0.0), axis=1, keepdims=True)


def dist(a, b):
    z, y = abs(a // 4 - b // 4), abs(a % 4 - b % 4)
    return min(z, 8 - z) + min(y, 4 - y)


def ordered(key):
    return [FIRST] + sorted([c for c in range(RANK) if c != FIRST], key=key)


ORDER_A = ordered(lambda chip: dist(chip, 0))
ORDER_C = ORDER_A


def in_order(x):
    place = [ORDER_A.index(chip) for chip in range(RANK)]
    pieces, start = [], 0
    for i in range(1, RANK + 1):
        if i == RANK or place[i] != place[i - 1] + 1:
            pieces.append(x[place[start] : place[start] + i - start])
            start = i
    return jnp.concatenate(pieces, axis=0) if len(pieces) > 1 else x


def spread_kernel(packet_ref, out_ref):
    pieces = [packet_ref[u : u + 1] for u in range(4)]
    pieces += [packet_ref[4 + s : 5 + s, :RANK] for s in range(4)]
    row = jnp.concatenate(pieces, axis=1)
    for d in range(out_ref.shape[0]):
        out_ref[d] = row


def contract_kernel(spectra_ref, gathered_ref, out_ref):
    scan = gathered_ref[:, :BINS]
    scan = in_order(scan)
    scan_high, scan_low = split(scan)
    stacked = jnp.concatenate([scan_high, scan_low], axis=0)
    last = gathered_ref.shape[0] - 1
    swapped = lax.axis_index("mz") == ORDER_A[-1]
    total = jnp.zeros((RANK, BINS), F32)
    gram = jnp.zeros((RANK, RANK), F32)
    for s in range(spectra_ref.shape[0]):
        one, two = (gathered_ref[d : d + 1, BINS + s * RANK : BINS + (s + 1) * RANK] for d in (0, last))
        one_column, two_column = as_column(one), as_column(two)
        gram = gram + (one_column * one + two_column * two)
        high, low = split(spectra_ref[s])
        both = jnp.dot(stacked, high, preferred_element_type=F32)
        part = both[:RANK] + both[RANK:] + jnp.dot(scan_high, low, preferred_element_type=F32)
        total = total + jnp.where(swapped, one_column, two_column) * part
    for t in range(TILES):
        out_ref[t * RANK : (t + 1) * RANK] = total[:, t * 128 : (t + 1) * 128]
    system = gram * nt_dot(scan, scan)
    out_ref[TILES * RANK :] = jnp.concatenate([system[8 * t : 8 * t + 8] for t in range(4)], axis=1)


def invert_kernel(total_ref, out_ref):
    system = total_ref[TILES * RANK :]
    tiles = RANK // 8
    columns = [
        [
            jnp.broadcast_to(system[:, RANK * t + j : RANK * t + j + 1], (8, 128))
            for t in range(tiles)
        ]
        for j in range(RANK)
    ]
    row, lane = iota((8, 128), 0), iota((8, 128), 1)
    work = [jnp.where(row + 8 * t == lane, 1.0, 0.0) for t in range(tiles)]
    pivots = [jnp.ones((8, 128), F32)] * tiles
    for k in range(RANK):
        top, r = divmod(k, 8)
        pivot = columns[k][top][r : r + 1]
        pivots[top] = jnp.where(row == r, pivot, pivots[top])
        scale = 1.0 / pivot
        factor = [columns[k][t] * scale if t >= top else None for t in range(tiles)]
        factor[top] = jnp.where(row > r, factor[top], 0.0)
        pivot_row = work[top][r : r + 1]
        for t in range(top, tiles):
            work[t] = work[t] - factor[t] * pivot_row
            for j in range(k + 1, min(8 * t + 8, RANK)):
                other = columns[k][j // 8][j % 8 : j % 8 + 1]
                columns[j][t] = columns[j][t] - factor[t] * other
    factor = jnp.concatenate(
        [(work[t] * lax.rsqrt(pivots[t]))[:, :RANK] for t in range(tiles)], axis=0
    )
    out_ref[...] = dot(factor.T, factor)


def solve_kernel(mine_ref, other_ref, inverse_ref, raw_ref, packet_ref):
    parts = [slice(t * RANK, (t + 1) * RANK) for t in range(TILES)]
    product = jnp.concatenate([mine_ref[part] + other_ref[part] for part in parts], axis=1)
    raw = dot(inverse_ref[...], product)
    slot, core = lax.axis_index("rt"), lax.axis_index("samp")
    tiles = [raw[:, t * 128 : (t + 1) * 128] for t in range(TILES)]
    own = jnp.where(
        slot < 2,
        jnp.where(slot == 0, tiles[0], tiles[1]),
        jnp.where(slot == 2, tiles[2], tiles[3]),
    )
    raw_ref[...] = jnp.where(core == 0, own, pltpu.roll(own, 64, 1))[:, :64]
    peak = jnp.max(jnp.abs(raw), axis=1, keepdims=True) + 1e-06
    high, low = split(raw * (1.0 / peak))
    both = nt_dot(jnp.concatenate([high, low], axis=0), high, None)
    gram = both[:RANK] + both[RANK:] + nt_dot(high, low, None)
    diagonal = iota((RANK, RANK), 0) == iota((RANK, RANK), 1)
    peak_row = jnp.sum(jnp.where(diagonal, peak, 0.0), axis=0, keepdims=True)
    row, column = iota((RANK, RANK), 0), iota((RANK, RANK), 1)
    within = (row >> 3) == (column >> 3)
    turned = jnp.concatenate([peak_row[:, 7:], peak_row[:, :7]], axis=1)
    gram = jnp.where(within & ((row & 7) == 7) & ((column & 7) < 7), peak_row, gram)
    gram = jnp.where(within & ((row & 7) == 6) & ((column & 7) == 0), turned, gram)
    blocks = jnp.concatenate([gram[8 * t : 8 * t + 8, 8 * t :] for t in range(4)], axis=1)
    packet = jnp.concatenate([blocks[u : u + 1] for u in range(8)], axis=1)
    for d in range(packet_ref.shape[0]):
        packet_ref[d] = packet


def take_lanes(x, lanes):
    return jnp.take_along_axis(x, lanes, axis=1, mode="promise_in_bounds")


def finish_kernel(packets_ref, raw_ref, factor_ref, peak_ref, gram_ref):
    width = 80
    component = iota((8, 128), 1) & (RANK - 1)
    offset = jnp.where(component < 8, 0, jnp.where(component < 16, 32, jnp.where(component < 24, 56, 72)))
    eighth = (component & 7) == 7
    place = jnp.where(eighth, jnp.maximum(offset - 32, 0), 48 + offset + (component & 7))
    peaks = []
    for d in range(0, packets_ref.shape[0], 8):
        first = take_lanes(packets_ref[d : d + 8, 384:512], jnp.full((8, 128), 96, jnp.int32))
        rest = take_lanes(packets_ref[d : d + 8, 512:], place)
        peaks.append(jnp.where(component == 7, first, rest))
    peaks = jnp.concatenate(peaks, axis=0)
    peak_row = jnp.max(peaks, axis=0, keepdims=True)
    ratio = peaks / peak_row
    tiles = []
    for t in range(5):
        place = iota((8, 128), 1) + 128 * t
        u, lane = place // width, place % width
        block = jnp.where(lane < 32, 0, jnp.where(lane < 56, 1, jnp.where(lane < 72, 2, 3)))
        column = jnp.where(
            lane < 32, lane, jnp.where(lane < 56, lane - 24, jnp.where(lane < 72, lane - 40, lane - 48))
        )
        total = jnp.zeros((8, 128), F32)
        for d in range(0, packets_ref.shape[0], 8):
            scale = ratio[d : d + 8]
            packet = packets_ref[d : d + 8, 128 * t : 128 * t + 128]
            total = total + packet * take_lanes(scale, 8 * block + u) * take_lanes(scale, column)
        tiles.append(jnp.sum(total, axis=0, keepdims=True))
    flat = jnp.concatenate(tiles, axis=1) * (1.0 / MZ)
    blocks = jnp.concatenate([flat[:, width * u : width * (u + 1)] for u in range(8)], axis=0)
    upper = jnp.concatenate(
        [
            blocks[:, :32],
            jnp.concatenate([jnp.zeros((8, 8), F32), blocks[:, 32:56]], axis=1),
            jnp.concatenate([jnp.zeros((8, 16), F32), blocks[:, 56:72]], axis=1),
            jnp.concatenate([jnp.zeros((8, 24), F32), blocks[:, 72:80]], axis=1),
        ],
        axis=0,
    )
    row, column = iota((RANK, RANK), 0), iota((RANK, RANK), 1)
    gram_ref[...] = jnp.where(row <= column, upper, upper.T)
    peak_ref[...] = peak_row[:, :RANK]
    factor_ref[...] = raw_ref[...] / as_column(peak_row[:, :RANK])


def call(kernel, shapes, ins, name=None):
    return pl.pallas_call(
        kernel,
        out_shape=[jax.ShapeDtypeStruct(s, F32) for s in shapes],
        in_specs=ins,
        out_specs=[VMEM] * len(shapes),
        compiler_params=pltpu.CompilerParams(vmem_limit_bytes=24 * 1024 * 1024),
        name=name,
    )


def shift(x, axis, size, by):
    return lax.ppermute(x, axis, [(i, (i + by) % size) for i in range(size)])


def swap(x, slots, core):
    pairs = [(i, i ^ (2 * slots + core)) for i in range(8)]
    return lax.ppermute(x, ("rt", "samp"), pairs)


def chip_groups(slots, mixed):
    order = ORDER_A if mixed else ORDER_C
    return [
        [
            (chip * slots + slot) * 2 + (1 - core if mixed and chip == order[-1] else core)
            for chip in order
        ]
        for slot in range(slots)
        for core in range(2)
    ]


def exchange(x, slots, mixed):
    groups = chip_groups(slots, mixed)
    return lax.all_to_all(x, ("mz", "rt", "samp"), 0, 0, axis_index_groups=groups)


def local(spectra, sample_factor, scan_factor):
    spectra_other = shift(spectra, "samp", 2, 1)
    sample = jnp.pad(sample_factor.T, ((0, 0), (0, 128 - RANK)))
    packet = jnp.concatenate([scan_factor.reshape(4, 128), sample], axis=0)
    width = BINS + 128
    (packets,) = call(spread_kernel, [(RANK, 1, width)], [VMEM], name="spread")(packet)
    gathered = exchange(packets, 4, True).reshape(RANK, width)
    (partial,) = call(contract_kernel, [(TILES * RANK + 8, 128)], [VMEM] * 2, name="contract")(
        spectra_other, gathered
    )
    two, three, one = (swap(partial, slots, core) for slots, core in ((2, 1), (3, 0), (1, 1)))
    mine = (partial + one) + (two + three)
    other = shift(mine, "samp", 2, 1)
    (inverse,) = call(invert_kernel, [(RANK, RANK)], [VMEM], name="invert")(mine)
    raw, packets = call(solve_kernel, [(RANK, 64), (RANK, 1, 640)], [VMEM] * 3, name="solve")(
        mine, other, inverse
    )
    packets = exchange(packets, 4, False).reshape(RANK, 640)
    factor, peak, gram = call(
        finish_kernel, [(RANK, 64), (1, RANK), (RANK, RANK)], [VMEM] * 2, name="finish"
    )(packets, raw)
    return (factor, peak.reshape(RANK), gram)


def solution(mesh):
    return jax.shard_map(
        local,
        mesh=mesh,
        in_specs=(P("samp", "rt", "mz"), P(None, "samp"), P("mz", "rt")),
        out_specs=(P(None, ("mz", "rt", "samp")), P(), P()),
        check_vma=False,
    )
```
